32 devices in a mesh: depth: 4 (over x, core), row: 4 (over z), col: 2 (over y).
Axes of the slice: x: 2, y: 2, z: 4, core: 2. Of those that a mesh axis runs over, the one named last changes fastest.
Arguments:
- density: float32 [4096, 4096], P('row', ('depth', 'col')), as said below
- pattern: int32 [64, 64], replicated, may hold values from 0 to 1, as said below
- filters: int32 [4, 64, 64], replicated, may hold values from 0 to 1, as said below
Outputs:
- purified: float32 [4096, 4096], P('row', ('depth', 'col'))
The draws below stay inside these ranges and needn't reach their ends.
Inputs may be any that keep to these rules, and one draw needn't show every extreme that they name: density is symmetric. `pattern`: symmetric 0/1 block table with every diagonal block set. `filters`: each table is a symmetric 0/1 block table with every diagonal block set.
All inputs are finite; a program needn't handle non-finite values.
Results may differ from the reference program's by a relative error of at most 0.007.
Values may be sent and summed in bfloat16 or wider, within the bound.
A program may use at most 64 MiB of HBM per device.

```python
import math
import jax
import jax.numpy as jnp

BLK = 64
NB = 64
PURIFY = 2
ORDER = 4096


def block_keep(key, near_pct, far_pct):
    tip_key, fill_key = jax.random.split(key)
    tip_block = jax.random.randint(tip_key, (), 0, NB)
    indices = jnp.arange(NB)
    closeby = jnp.abs(indices - tip_block) < max(NB // 4, 1)
    nearby = closeby[:, None] & closeby[None, :] | (jnp.abs(indices[:, None] - indices[None, :]) <= 2)
    rolled = jax.random.randint(fill_key, (NB, NB), 0, 100)
    kept_blocks = rolled < jnp.where(nearby, near_pct, far_pct)
    kept_blocks = kept_blocks | kept_blocks.T | (indices[:, None] == indices[None, :])
    return kept_blocks.astype(jnp.int32)


def draw_pattern(key, part):
    return block_keep(jax.random.fold_in(key, 11), 90, 45)


def draw_filters(key, part):
    tables = [block_keep(jax.random.fold_in(key, 100 + number), 97, 70) for number in range(2 * PURIFY)]
    return jnp.stack(tables)


def draw_density(key, part):
    noise_key, diag_key = jax.random.split(jax.random.fold_in(key, 7), 2)
    indices = jnp.arange(ORDER)
    random_part = jax.random.normal(noise_key, (ORDER, ORDER), jnp.float32)
    diagonal = jax.random.uniform(diag_key, (ORDER,), jnp.float32, 0.25, 0.75)
    symmetric = (random_part + random_part.T) * (0.25 / math.sqrt(2.0 * ORDER))
    return jnp.where(indices[:, None] == indices[None, :], diagonal[:, None], symmetric)


def setup_inputs(seed: int = 0) -> dict:
    seeds = jax.random.split(jax.random.key(seed), 4)
    return {
        "density": draw_density(jax.random.fold_in(seeds[3], 71), 0),
        "pattern": draw_pattern(jax.random.fold_in(seeds[3], 71), 0),
        "filters": draw_filters(jax.random.fold_in(seeds[3], 71), 0),
    }


def expand(keep_table):
    shaped = jnp.broadcast_to(keep_table.astype(jnp.float32)[:, None, :, None], (NB, BLK, NB, BLK))
    return shaped.reshape(ORDER, ORDER)


def reference(density, pattern, filters):
    current = density * expand(pattern)
    for round_index in range(PURIFY):
        operand = current.astype(jnp.bfloat16)
        square = jnp.dot(operand, operand, preferred_element_type=jnp.float32) * expand(filters[2 * round_index])
        cubic = jnp.dot(square.astype(jnp.bfloat16), operand, preferred_element_type=jnp.float32) * expand(filters[2 * round_index + 1])
        current = 3.0 * square - 2.0 * cubic
    return current
```

```python
import functools

import jax
import jax.numpy as jnp
from jax import lax
from jax.experimental import pallas as pl
from jax.experimental.pallas import tpu as pltpu
from jax.sharding import PartitionSpec as P

BLK = 64
PURIFY = 2
CORES = 2
MESH = pl.DeviceIdType.MESH


def kernel(dims, dens, tabs, out, a_row, a_col, s_row, sq, acc, mask,
           z_send, z_recv, a_send, a_recv, af_send, af_recv,
           s_send, s_recv, sf_send, sf_recv):
    nd, nr, nc, h, w, cw, tm = dims
    Q = w // cw
    nx = nd // CORES
    m = h // w
    rb, sb = h // BLK, w // BLK
    d, r, c = lax.axis_index("depth"), lax.axis_index("row"), lax.axis_index("col")
    x, core = d // CORES, d % CORES
    sib = x * CORES + (1 - core)
    me = d * nc + c
    peers = [(px, pc) for px in range(nx) for pc in range(nc) if px or pc]

    def dev(dd, rr, cc):
        return (dd, rr, cc)

    def peer_to(p):
        px, pc = peers[p]
        return ((x + px) % nx) * CORES + core, (c + pc) % nc

    def peer_from(p, k):
        px, pc = peers[p]
        return ((x + nx - px) % nx) * CORES + k, (c + nc - pc) % nc

    bar = pltpu.get_barrier_semaphore()
    for p in range(len(peers)):
        dd, cc = peer_to(p)
        pl.semaphore_signal(bar, inc=1, device_id=dev(dd, r, cc), device_id_type=MESH)
    pl.semaphore_signal(bar, inc=1, device_id=dev(sib, r, c), device_id_type=MESH)

    @pl.when(r > 0)
    def _():
        pl.semaphore_signal(bar, inc=1, device_id=dev(d, r - 1, c), device_id_type=MESH)

    @pl.when(r < nr - 1)
    def _():
        pl.semaphore_signal(bar, inc=1, device_id=dev(d, r + 1, c), device_id_type=MESH)

    tb = tm // BLK
    slot = lax.broadcasted_iota(jnp.int32, (h // tm * 8, tabs.shape[1]), 0)
    r_pick = (slot // 8 * tb + slot % 8 + r * rb
              == lax.broadcasted_iota(jnp.int32, (h // tm * 8, tabs.shape[1]), 1)).astype(jnp.float32)
    c_pick = ((lax.broadcasted_iota(jnp.int32, (tabs.shape[2], w), 1) // BLK + me * sb)
              == lax.broadcasted_iota(jnp.int32, (tabs.shape[2], w), 0)).astype(jnp.float32)
    for k in range(tabs.shape[0]):
        rows = jnp.dot(r_pick, tabs[k].astype(jnp.float32), preferred_element_type=jnp.float32)
        mask[k] = jnp.dot(rows, c_pick, preferred_element_type=jnp.float32)

    def tile_mask(k, t, q):
        mk = mask[k, pl.ds(pl.multiple_of(t * 8, 8), 8), q * cw:(q + 1) * cw][:tb]
        return jnp.broadcast_to(mk[:, None, :], (tb, BLK, cw)).reshape(tm, cw)

    def rows_of(t):
        return pl.ds(pl.multiple_of(t * tm, tm), tm)

    @pl.loop(0, h // tm)
    def _(t):
        for q in range(Q):
            v = (dens[rows_of(t), q * cw:(q + 1) * cw] * tile_mask(0, t, q)).astype(jnp.bfloat16)
            a_col[0, r, q, rows_of(t), :] = v
            a_row[0, me, q, rows_of(t), :] = v

    near = jnp.minimum(r, 1) + jnp.minimum(nr - 1 - r, 1)
    for n in range(3):
        @pl.when(near == n)
        def _():
            pl.semaphore_wait(bar, len(peers) + 1 + n)

    def z_copy(s, q, src, up):
        ref = a_col.at[s, src, q]
        return pltpu.make_async_remote_copy(
            src_ref=ref, dst_ref=ref, send_sem=z_send.at[s, q, src, up],
            recv_sem=z_recv.at[s, q, src],
            device_id=dev(d, r + 1 if up else r - 1, c), device_id_type=MESH)

    def z_own(s, q, op):
        @pl.when(r < nr - 1)
        def _():
            getattr(z_copy(s, q, r, 1), op)()

        @pl.when(r > 0)
        def _():
            getattr(z_copy(s, q, r, 0), op)()

    def z_arrive(s, q, dist):
        @pl.when(r + dist < nr)
        def _():
            z_copy(s, q, r + dist, 1).wait_recv()

            @pl.when(r > 0)
            def _():
                z_copy(s, q, r + dist, 0).start()

        @pl.when(r - dist >= 0)
        def _():
            z_copy(s, q, r - dist, 0).wait_recv()

            @pl.when(r < nr - 1)
            def _():
                z_copy(s, q, r - dist, 1).start()

    def z_drain(s, q):
        z_own(s, q, "wait_send")
        for dist in range(1, nr - 1):
            @pl.when((r + dist < nr) & (r > 0))
            def _():
                z_copy(s, q, r + dist, 0).wait_send()

            @pl.when((r - dist >= 0) & (r < nr - 1))
            def _():
                z_copy(s, q, r - dist, 1).wait_send()

    def ac(ref, ss, rs, to):
        return pltpu.make_async_remote_copy(
            src_ref=ref, dst_ref=ref, send_sem=ss, recv_sem=rs,
            device_id=dev(to[0], r, to[1]), device_id_type=MESH)

    class Gather:
        def __init__(self, view, send, recv, fsend, frecv):
            self.view, self.send, self.recv = view, send, recv
            self.fsend, self.frecv = fsend, frecv

        def own(self, p):
            return ac(self.view(me), self.send(p), self.recv(p), peer_to(p))

        def got(self, p):
            dd, cc = peer_from(p, core)
            return ac(self.view(dd * nc + cc), self.send(p), self.recv(p), peer_to(p))

        def fwd(self, p):
            if p == len(peers):
                return ac(self.view(me), self.fsend(p), self.frecv(p), (sib, c))
            dd, cc = peer_from(p, core)
            return ac(self.view(dd * nc + cc), self.fsend(p), self.frecv(p), (sib, c))

        def fgot(self, p):
            if p == len(peers):
                dd, cc = sib, c
            else:
                dd, cc = peer_from(p, 1 - core)
            return ac(self.view(dd * nc + cc), self.fsend(p), self.frecv(p), (sib, c))

        def begin(self):
            for p in range(len(peers)):
                self.own(p).start()
            self.fwd(len(peers)).start()

        def relay(self):
            for p in range(len(peers)):
                self.got(p).wait_recv()
                self.fwd(p).start()

        def finish(self):
            for p in range(len(peers) + 1):
                self.fgot(p).wait_recv()

        def drain(self):
            for p in range(len(peers)):
                self.own(p).wait_send()
            for p in range(len(peers) + 1):
                self.fwd(p).wait_send()

    ga = [Gather(lambda j, s=s: a_row.at[s, j], lambda p, s=s: a_send.at[s, p],
                 lambda p, s=s: a_recv.at[s, p], lambda p, s=s: af_send.at[s, p],
                 lambda p, s=s: af_recv.at[s, p]) for s in range(PURIFY)]
    gs = [[Gather(lambda j, s=s, q=q: s_row.at[s, j, q], lambda p, s=s, q=q: s_send.at[s, q, p],
                  lambda p, s=s, q=q: s_recv.at[s, q, p], lambda p, s=s, q=q: sf_send.at[s, q, p],
                  lambda p, s=s, q=q: sf_recv.at[s, q, p]) for q in range(Q)] for s in range(PURIFY)]

    def square(s, q):
        @pl.loop(0, h // tm)
        def _(t):
            tot = None
            for j in range(nd * nc):
                for k in range(Q):
                    lo = (j % m) * w + k * cw
                    part = jnp.dot(a_row[s, j, k, rows_of(t), :],
                                   a_col[s, j // m, q, lo:lo + cw, :],
                                   preferred_element_type=jnp.float32)
                    tot = part if tot is None else tot + part
            tot = tot * tile_mask(2 * s + 1, t, q)
            sq[q, rows_of(t), :] = tot
            s_row[s, me, q, rows_of(t), :] = tot.astype(jnp.bfloat16)

    def cubic(s, k):
        @pl.loop(0, h // tm)
        def _(t):
            for q in range(Q):
                tot = None if k == 0 else acc[q, rows_of(t), :]
                for j in range(nd * nc):
                    lo = (j % m) * w + k * cw
                    part = jnp.dot(s_row[s, j, k, rows_of(t), :],
                                   a_col[s, j // m, q, lo:lo + cw, :],
                                   preferred_element_type=jnp.float32)
                    tot = part if tot is None else tot + part
                if k < Q - 1:
                    acc[q, rows_of(t), :] = tot
                else:
                    cur = 3.0 * sq[q, rows_of(t), :] - 2.0 * (tot * tile_mask(2 * s + 2, t, q))
                    if s < PURIFY - 1:
                        v = cur.astype(jnp.bfloat16)
                        a_col[s + 1, r, q, rows_of(t), :] = v
                        a_row[s + 1, me, q, rows_of(t), :] = v
                    else:
                        out[rows_of(t), q * cw:(q + 1) * cw] = cur

    for s in range(PURIFY):
        z_own(s, 0, "start")
        ga[s].begin()
        for q in range(Q):
            for dist in range(1, nr):
                z_arrive(s, q, dist)
                if q + 1 < Q and dist == min(2, nr - 1):
                    z_own(s, q + 1, "start")
            if q == 0:
                ga[s].relay()
                ga[s].finish()
            square(s, q)
            gs[s][q].begin()
        for k in range(Q):
            gs[s][k].relay()
            gs[s][k].finish()
            cubic(s, k)
    for s in range(PURIFY):
        ga[s].drain()
        for q in range(Q):
            z_drain(s, q)
            gs[s][q].drain()


def on_device(dims, density, pattern, filters):
    nd, nr, nc, h, w, cw, tm = dims
    Q = w // cw
    J = nd * nc
    n_peers = J // CORES - 1
    tabs = jnp.concatenate([pattern[None], filters], 0)
    dma = pltpu.SemaphoreType.DMA
    return pl.pallas_call(
        functools.partial(kernel, dims),
        out_shape=jax.ShapeDtypeStruct((h, w), jnp.float32),
        in_specs=[pl.BlockSpec(memory_space=pltpu.VMEM)] * 2,
        out_specs=pl.BlockSpec(memory_space=pltpu.VMEM),
        scratch_shapes=[
            pltpu.VMEM((PURIFY, J, Q, h, cw), jnp.bfloat16),
            pltpu.VMEM((PURIFY, nr, Q, h, cw), jnp.bfloat16),
            pltpu.VMEM((PURIFY, J, Q, h, cw), jnp.bfloat16),
            pltpu.VMEM((Q, h, cw), jnp.float32),
            pltpu.VMEM((Q, h, cw), jnp.float32),
            pltpu.VMEM((2 * PURIFY + 1, h // tm * 8, w), jnp.float32),
            dma((PURIFY, Q, nr, 2)), dma((PURIFY, Q, nr)),
            dma((PURIFY, n_peers)), dma((PURIFY, n_peers)),
            dma((PURIFY, n_peers + 1)), dma((PURIFY, n_peers + 1)),
            dma((PURIFY, Q, n_peers)), dma((PURIFY, Q, n_peers)),
            dma((PURIFY, Q, n_peers + 1)), dma((PURIFY, Q, n_peers + 1)),
        ],
        compiler_params=pltpu.CompilerParams(
            collective_id=0, has_side_effects=True, vmem_limit_bytes=62 * 2 ** 20),
    )(density, tabs)


def solution(mesh):
    nd, nr, nc = mesh.shape["depth"], mesh.shape["row"], mesh.shape["col"]

    def run(density, pattern, filters):
        h, w = density.shape
        cw = 256 if w % 256 == 0 else w
        tm = 256 if h % 256 == 0 else h
        return on_device((nd, nr, nc, h, w, cw, tm), density, pattern, filters)

    return jax.shard_map(
        run,
        mesh=mesh,
        in_specs=(P("row", ("depth", "col")), P(), P()),
        out_specs=P("row", ("depth", "col")),
        check_vma=False,
    )
```

```python
import functools

import jax
import jax.numpy as jnp
from jax import lax
from jax.experimental import pallas as pl
from jax.experimental.pallas import tpu as pltpu
from jax.sharding import PartitionSpec as P

BLK = 64
PURIFY = 2
CORES = 2
LANES = 128
MESH = pl.DeviceIdType.MESH


def kernel(dims, dens, tabs, out, a_row, a_col, s_row, sq, acc, mask,
           z_send, z_recv, a_send, a_recv, af_send, af_recv,
           s_send, s_recv, sf_send, sf_recv):
    nd, nr, nc, h, w, tm, cuts = dims
    Q = len(cuts)
    G = w // LANES
    nx = nd // CORES
    m = h // w
    rb, sb = h // BLK, w // BLK
    d, r, c = lax.axis_index("depth"), lax.axis_index("row"), lax.axis_index("col")
    x, core = d // CORES, d % CORES
    sib = x * CORES + (1 - core)
    me = d * nc + c
    peers = [(px, pc) for px in range(nx) for pc in range(nc) if px or pc]
    direct = [p for p, (px, pc) in enumerate(peers) if not (px and pc)]
    bent = [p for p, (px, pc) in enumerate(peers) if px and pc]

    def dev(dd, rr, cc):
        return (dd, rr, cc)

    def peer_to(p):
        px, pc = peers[p]
        return ((x + px) % nx) * CORES + core, (c + pc) % nc

    def peer_from(p, k):
        px, pc = peers[p]
        return ((x + nx - px) % nx) * CORES + k, (c + nc - pc) % nc

    bar = pltpu.get_barrier_semaphore()
    for p in direct:
        dd, cc = peer_to(p)
        pl.semaphore_signal(bar, inc=1, device_id=dev(dd, r, cc), device_id_type=MESH)
    pl.semaphore_signal(bar, inc=1, device_id=dev(sib, r, c), device_id_type=MESH)

    @pl.when(r > 0)
    def _():
        pl.semaphore_signal(bar, inc=1, device_id=dev(d, r - 1, c), device_id_type=MESH)

    @pl.when(r < nr - 1)
    def _():
        pl.semaphore_signal(bar, inc=1, device_id=dev(d, r + 1, c), device_id_type=MESH)

    tb = tm // BLK
    slot = lax.broadcasted_iota(jnp.int32, (h // tm * 8, tabs.shape[1]), 0)
    r_pick = (slot // 8 * tb + slot % 8 + r * rb
              == lax.broadcasted_iota(jnp.int32, (h // tm * 8, tabs.shape[1]), 1)).astype(jnp.float32)
    c_pick = ((lax.broadcasted_iota(jnp.int32, (tabs.shape[2], w), 1) // BLK + me * sb)
              == lax.broadcasted_iota(jnp.int32, (tabs.shape[2], w), 0)).astype(jnp.float32)
    for k in range(tabs.shape[0]):
        rows = jnp.dot(r_pick, tabs[k].astype(jnp.float32), preferred_element_type=jnp.float32)
        mask[k] = jnp.dot(rows, c_pick, preferred_element_type=jnp.float32)

    def tile_mask(k, t, g0, g1):
        n = (g1 - g0) * LANES
        mk = mask[k, pl.ds(pl.multiple_of(t * 8, 8), 8), g0 * LANES:g1 * LANES][:tb]
        return jnp.broadcast_to(mk[:, None, :], (tb, BLK, n)).reshape(tm, n)

    def rows_of(t):
        return pl.ds(pl.multiple_of(t * tm, tm), tm)

    @pl.loop(0, h // tm)
    def _(t):
        for g in range(G):
            v = (dens[rows_of(t), g * LANES:(g + 1) * LANES] * tile_mask(0, t, g, g + 1)).astype(jnp.bfloat16)
            a_col[0, r, g, rows_of(t), :] = v
            a_row[0, me, g, rows_of(t), :] = v

    near = jnp.minimum(r, 1) + jnp.minimum(nr - 1 - r, 1)
    for n in range(3):
        @pl.when(near == n)
        def _():
            pl.semaphore_wait(bar, len(direct) + 1 + n)

    def z_copy(s, q, src, up):
        ref = a_col.at[s, src, cuts[q][0]:cuts[q][1]]
        return pltpu.make_async_remote_copy(
            src_ref=ref, dst_ref=ref, send_sem=z_send.at[s, q, src, up],
            recv_sem=z_recv.at[s, q, src],
            device_id=dev(d, r + 1 if up else r - 1, c), device_id_type=MESH)

    def z_own(s, q, op):
        @pl.when(r < nr - 1)
        def _():
            getattr(z_copy(s, q, r, 1), op)()

        @pl.when(r > 0)
        def _():
            getattr(z_copy(s, q, r, 0), op)()

    def z_arrive(s, q, dist):
        @pl.when(r + dist < nr)
        def _():
            z_copy(s, q, r + dist, 1).wait_recv()

            @pl.when(r > 0)
            def _():
                z_copy(s, q, r + dist, 0).start()

        @pl.when(r - dist >= 0)
        def _():
            z_copy(s, q, r - dist, 0).wait_recv()

            @pl.when(r < nr - 1)
            def _():
                z_copy(s, q, r - dist, 1).start()

    def z_drain(s, q):
        z_own(s, q, "wait_send")
        for dist in range(1, nr - 1):
            @pl.when((r + dist < nr) & (r > 0))
            def _():
                z_copy(s, q, r + dist, 0).wait_send()

            @pl.when((r - dist >= 0) & (r < nr - 1))
            def _():
                z_copy(s, q, r - dist, 1).wait_send()

    def ac(ref, ss, rs, to):
        return pltpu.make_async_remote_copy(
            src_ref=ref, dst_ref=ref, send_sem=ss, recv_sem=rs,
            device_id=dev(to[0], r, to[1]), device_id_type=MESH)

    class Gather:
        def __init__(self, view, send, recv, fsend, frecv):
            self.view, self.send, self.recv = view, send, recv
            self.fsend, self.frecv = fsend, frecv

        def block(self, p, k):
            dd, cc = peer_from(p, k)
            return self.view(dd * nc + cc)

        def half(self, dd, cc, i):
            return self.view(dd * nc + cc).at[:, i * (h // 2):(i + 1) * (h // 2), :]

        def own(self, p):
            return ac(self.view(me), self.send(p, 0), self.recv(p, 0), peer_to(p))

        def got(self, p, i=None):
            if i is None:
                return ac(self.block(p, core), self.send(p, 0), self.recv(p, 0), peer_to(p))
            dd, cc = peer_from(p, core)
            return ac(self.half(dd, cc, i), self.send(p, i), self.recv(p, i), peer_to(p))

        def turn(self, p, i):
            px, pc = peers[p]
            if i == 0:
                ref = self.half(((x + nx - px) % nx) * CORES + core, c, 0)
                to = (d, (c + pc) % nc)
            else:
                ref = self.half(d, (c + nc - pc) % nc, 1)
                to = (((x + px) % nx) * CORES + core, c)
            return ac(ref, self.send(p, i), self.recv(p, i), to)

        def fwd(self, p):
            ref = self.view(me) if p == len(peers) else self.block(p, core)
            return ac(ref, self.fsend(p), self.frecv(p), (sib, c))

        def fgot(self, p):
            ref = self.view(sib * nc + c) if p == len(peers) else self.block(p, 1 - core)
            return ac(ref, self.fsend(p), self.frecv(p), (sib, c))

        def begin(self):
            for p in direct:
                self.own(p).start()
            self.fwd(len(peers)).start()

        def hop(self):
            for q in direct:
                self.got(q).wait_recv()
                for p in bent:
                    if peers[q] == (peers[p][0], 0):
                        self.turn(p, 0).start()
                    if peers[q] == (0, peers[p][1]):
                        self.turn(p, 1).start()
            for q in direct:
                self.fwd(q).start()

        def relay(self):
            for p in bent:
                self.got(p, 0).wait_recv()
                self.got(p, 1).wait_recv()
                self.fwd(p).start()

        def finish(self):
            for p in range(len(peers) + 1):
                self.fgot(p).wait_recv()

        def drain(self):
            for p in direct:
                self.own(p).wait_send()
            for p in bent:
                self.turn(p, 0).wait_send()
                self.turn(p, 1).wait_send()
            for p in range(len(peers) + 1):
                self.fwd(p).wait_send()

    ga = [Gather(lambda j, s=s: a_row.at[s, j], lambda p, i, s=s: a_send.at[s, p, i],
                 lambda p, i, s=s: a_recv.at[s, p, i], lambda p, s=s: af_send.at[s, p],
                 lambda p, s=s: af_recv.at[s, p]) for s in range(PURIFY)]
    gs = [[Gather(lambda j, s=s, q=q: s_row.at[s, j, cuts[q][0]:cuts[q][1]],
                  lambda p, i, s=s, q=q: s_send.at[s, q, p, i],
                  lambda p, i, s=s, q=q: s_recv.at[s, q, p, i],
                  lambda p, s=s, q=q: sf_send.at[s, q, p],
                  lambda p, s=s, q=q: sf_recv.at[s, q, p]) for q in range(Q)] for s in range(PURIFY)]

    def product(left, s, t, groups, g0, g1):
        cells = [(j, g) for j in range(nd * nc) for g in groups]
        tot = None
        for i in range(0, len(cells), 2):
            pair = cells[i:i + 2]
            lhs = jnp.concatenate([left[s, j, g, rows_of(t), :] for j, g in pair], axis=1)
            cols = []
            for n in range(g0, g1):
                los = [(j // m, (j % m) * w + g * LANES) for j, g in pair]
                if len(los) == 2 and los[1] == (los[0][0], los[0][1] + LANES):
                    cols.append(a_col[s, los[0][0], n, los[0][1]:los[0][1] + 2 * LANES, :])
                else:
                    cols.append(jnp.concatenate([a_col[s, b, n, lo:lo + LANES, :] for b, lo in los], axis=0))
            part = jnp.dot(lhs, jnp.concatenate(cols, axis=1), preferred_element_type=jnp.float32)
            tot = part if tot is None else tot + part
        return tot

    def square(s, q):
        g0, g1 = cuts[q]

        @pl.loop(0, h // tm)
        def _(t):
            tot = product(a_row, s, t, range(G), g0, g1) * tile_mask(2 * s + 1, t, g0, g1)
            sq[rows_of(t), g0 * LANES:g1 * LANES] = tot
            v = tot.astype(jnp.bfloat16)
            for g in range(g0, g1):
                s_row[s, me, g, rows_of(t), :] = v[:, (g - g0) * LANES:(g - g0 + 1) * LANES]

    def cubic(s, k, g0, g1):
        cols = slice(g0 * LANES, g1 * LANES)

        @pl.loop(0, h // tm)
        def _(t):
            tot = product(s_row, s, t, range(*cuts[k]), g0, g1)
            if k > 0:
                tot = tot + acc[rows_of(t), cols]
            if k < Q - 1:
                acc[rows_of(t), cols] = tot
                return
            cur = 3.0 * sq[rows_of(t), cols] - 2.0 * (tot * tile_mask(2 * s + 2, t, g0, g1))
            if s < PURIFY - 1:
                v = cur.astype(jnp.bfloat16)
                for g in range(g0, g1):
                    part = v[:, (g - g0) * LANES:(g - g0 + 1) * LANES]
                    a_col[s + 1, r, g, rows_of(t), :] = part
                    a_row[s + 1, me, g, rows_of(t), :] = part
            else:
                out[rows_of(t), cols] = cur

    wide = [(g, min(g + 2, G)) for g in range(0, G, 2)]
    for s in range(PURIFY):
        if s == 0:
            z_own(s, 0, "start")
        ga[s].begin()
        for q in range(Q):
            for dist in range(1, nr):
                z_arrive(s, q, dist)
                if q + 1 < Q and dist == min(2, nr - 1):
                    z_own(s, q + 1, "start")
                if q == 0 and dist == min(2, nr - 1):
                    ga[s].hop()
            if q == 0:
                ga[s].relay()
                ga[s].finish()
            if q >= 2:
                gs[s][q - 2].relay()
            if q >= 1:
                gs[s][q - 1].hop()
            square(s, q)
            gs[s][q].begin()
        if Q >= 2:
            gs[s][Q - 2].relay()
        for k in range(Q):
            if k == max(Q - 2, 0):
                gs[s][Q - 1].hop()
            if k == Q - 1:
                gs[s][k].relay()
            gs[s][k].finish()
            for i, (g0, g1) in enumerate(wide):
                cubic(s, k, g0, g1)
                if k == Q - 1 and s < PURIFY - 1 and g1 == cuts[0][1]:
                    z_own(s + 1, 0, "start")
    for s in range(PURIFY):
        ga[s].drain()
        for q in range(Q):
            z_drain(s, q)
            gs[s][q].drain()


def on_device(dims, density, pattern, filters):
    nd, nr, nc, h, w, tm, cuts = dims
    Q = len(cuts)
    G = w // LANES
    J = nd * nc
    n_peers = J // CORES - 1
    tabs = jnp.concatenate([pattern[None], filters], 0)
    dma = pltpu.SemaphoreType.DMA
    return pl.pallas_call(
        functools.partial(kernel, dims),
        out_shape=jax.ShapeDtypeStruct((h, w), jnp.float32),
        in_specs=[pl.BlockSpec(memory_space=pltpu.VMEM)] * 2,
        out_specs=pl.BlockSpec(memory_space=pltpu.VMEM),
        scratch_shapes=[
            pltpu.VMEM((PURIFY, J, G, h, LANES), jnp.bfloat16),
            pltpu.VMEM((PURIFY, nr, G, h, LANES), jnp.bfloat16),
            pltpu.VMEM((PURIFY, J, G, h, LANES), jnp.bfloat16),
            pltpu.VMEM((h, w), jnp.float32),
            pltpu.VMEM((h, w), jnp.float32),
            pltpu.VMEM((2 * PURIFY + 1, h // tm * 8, w), jnp.float32),
            dma((PURIFY, Q, nr, 2)), dma((PURIFY, Q, nr)),
            dma((PURIFY, n_peers, 2)), dma((PURIFY, n_peers, 2)),
            dma((PURIFY, n_peers + 1)), dma((PURIFY, n_peers + 1)),
            dma((PURIFY, Q, n_peers, 2)), dma((PURIFY, Q, n_peers, 2)),
            dma((PURIFY, Q, n_peers + 1)), dma((PURIFY, Q, n_peers + 1)),
        ],
        compiler_params=pltpu.CompilerParams(
            collective_id=0, has_side_effects=True, vmem_limit_bytes=62 * 2 ** 20),
    )(density, tabs)


def solution(mesh):
    nd, nr, nc = mesh.shape["depth"], mesh.shape["row"], mesh.shape["col"]

    def run(density, pattern, filters):
        h, w = density.shape
        tm = 256 if h % 256 == 0 else h
        groups = w // LANES
        cuts = [(g, g + 1) for g in range(groups)]
        if groups >= 4:
            cuts = [(g, g + 2) for g in range(0, groups - 2, 2)] + cuts[groups - 2:]
        return on_device((nd, nr, nc, h, w, tm, tuple(cuts)), density, pattern, filters)

    return jax.shard_map(
        run,
        mesh=mesh,
        in_specs=(P("row", ("depth", "col")), P(), P()),
        out_specs=P("row", ("depth", "col")),
        check_vma=False,
    )
```
